32 devices in a mesh: seq: 16 (over z, y, core), tp: 2 (over x).
Axes of the slice: x: 2, y: 2, z: 4, core: 2. Of those that a mesh axis runs over, the one named last changes fastest.
Arguments:
- q_raw: bfloat16 [1024, 5120], P('seq', 'tp'), may hold values from -160 to 160
- k_raw: bfloat16 [1024, 5120], P('seq', 'tp'), may hold values from -160 to 160
- v_new: bfloat16 [1024, 5120], P('seq', 'tp'), may hold values from -8 to 8
- q_gain: float32 [5120], P('tp'), may hold values from 1.5 to 3
- k_gain: float32 [5120], P('tp'), may hold values from 1 to 2
- cache_keys: bfloat16 [512, 128, 5120], P('seq', None, 'tp'), may hold values from -10 to 10
- cache_values: bfloat16 [512, 128, 5120], P('seq', None, 'tp'), may hold values from -8 to 8
- page_table: int32 [2, 256], replicated, may hold values from 0 to 511, as said below
- cached_lengths: int32 [2], replicated, may hold values from 6553 to 32768, as said below
- req_group: int32 [4], replicated, may hold values from 0 to 1, as said below
Outputs:
- attended: bfloat16 [1024, 5120], P('seq', 'tp')
The draws below stay inside these ranges and needn't reach their ends.
Inputs may be any that keep to these rules, and one draw needn't show every extreme that they name: `page_table`: the 256 pages of group g lie on distinct slots s with (s // 16) % 2 == g; every slot holds one page. `cached_lengths`: one group's length is exactly 32768. `req_group`: exactly 2 requests belong to each group.
All inputs are finite; a program needn't handle non-finite values.
Results may differ from the reference program's by a relative error of at most 0.013.
Values may be sent and summed in bfloat16 or wider, within the bound.
A program may use at most 256 MiB of HBM per device.

```python
import math
import jax
import jax.numpy as jnp
from jax import lax

HEADS = 40
HDIM = 128
D = 5120
GROUPS = 2
PAGE = 128
CACHE_PAGES = 256
NEWTOK = 256
TOKENS = 1024
REQ = 4
GP_DEV = 16


def scaled_rows(key, salt):
    first, second, third = jax.random.split(jax.random.fold_in(key, salt), 3)
    columns = 3.0 ** (jnp.arange(D, dtype=jnp.float32) / (D - 1))
    columns = columns * jax.random.uniform(third, (D,), minval=0.8, maxval=1.25)
    row_scale = 10.0 ** jax.random.uniform(second, (TOKENS, 1))
    base = jax.random.truncated_normal(first, -4.0, 4.0, (TOKENS, D))
    return base * row_scale * columns


def draw_q_raw(key, part):
    values = scaled_rows(key, 11)
    return values.astype(jnp.bfloat16)


def draw_k_raw(key, part):
    return scaled_rows(key, 12).astype(jnp.bfloat16)


def draw_cache_keys(key, part):
    slot_count = GROUPS * CACHE_PAGES
    first = jax.random.fold_in(jax.random.fold_in(key, 31), 0)
    base = jax.random.truncated_normal(first, -6.0, 6.0, (slot_count, PAGE, D))
    return base.astype(jnp.bfloat16)


def draw_page_table(key, part):
    subkeys = jax.random.split(jax.random.fold_in(key, 21), GROUPS)
    orders = jax.vmap(lambda sub: jax.random.permutation(sub, CACHE_PAGES))(subkeys).astype(jnp.int32)
    group_ids = jnp.arange(GROUPS, dtype=jnp.int32)[:, None]
    slots = orders // GP_DEV * (GROUPS * GP_DEV) + group_ids * GP_DEV + orders % GP_DEV
    return slots.astype(jnp.int32)


def draw_cached_lengths(key, part):
    first, second = jax.random.split(jax.random.fold_in(key, 51))
    capacity = CACHE_PAGES * PAGE
    shorter = jax.random.randint(first, (GROUPS,), capacity // 5, 2 * capacity // 5 + 1)
    longest = jax.random.randint(second, (), 0, GROUPS)
    lengths = jnp.where(jnp.arange(GROUPS) == longest, capacity, shorter)
    return lengths.astype(jnp.int32)


def draw_req_group(key, part):
    order = jax.random.permutation(jax.random.fold_in(key, 41), REQ)
    return (order % GROUPS).astype(jnp.int32)


def level_of(rng, extent, cuts, smallest, high):
    def one(position, blocks):
        heights = jax.random.uniform(jax.random.fold_in(jax.random.fold_in(rng, 6), position), (blocks,), jnp.float32, smallest / len(cuts), high / len(cuts))
        return jnp.repeat(jnp.exp(heights), extent[position] // blocks).reshape((-1,) + (1,) * (len(extent) - position - 1))

    loudness = one(*cuts[0])
    for cut in cuts[1:]:
        loudness = loudness * one(*cut)
    return loudness


def normal_values(stream_key, dims, spread, most, shards=(), kind=jnp.bfloat16):
    drawn = spread * jax.random.normal(stream_key, dims, jnp.float32)
    if shards:
        drawn = drawn * level_of(stream_key, dims, shards, -0.22, 0.18)
    return jnp.clip(drawn, -most, most).astype(kind)


def setup_inputs(seed: int = 0) -> dict:
    key_list = jax.random.split(jax.random.key(seed), 11)
    q_raw = draw_q_raw(jax.random.fold_in(key_list[10], 71), 0)
    k_raw = draw_k_raw(jax.random.fold_in(key_list[10], 71), 0)
    v_new = normal_values(key_list[2], (TOKENS, D), 2.0, 8.0, ((0, 16), (1, 2)))
    q_gain = jnp.clip(1.5 + 1.5 * jax.random.uniform(key_list[3], (D,), jnp.float32) ** level_of(key_list[3], (D,), ((0, 2),), -0.2, 0.2), 1.5, 3.0)
    k_gain = jnp.clip(1.0 + 1.0 * jax.random.uniform(key_list[4], (D,), jnp.float32) ** level_of(key_list[4], (D,), ((0, 2),), -0.2, 0.2), 1.0, 2.0)
    cache_keys = draw_cache_keys(jax.random.fold_in(key_list[10], 71), 0)
    cache_values = normal_values(key_list[6], (GROUPS * CACHE_PAGES, PAGE, D), 2.0, 8.0, ((0, 16), (2, 2)))
    page_table = draw_page_table(jax.random.fold_in(key_list[10], 71), 0)
    cached_lengths = draw_cached_lengths(jax.random.fold_in(key_list[10], 71), 0)
    req_group = draw_req_group(jax.random.fold_in(key_list[10], 71), 0)
    return {"q_raw": q_raw, "k_raw": k_raw, "v_new": v_new, "q_gain": q_gain, "k_gain": k_gain, "cache_keys": cache_keys, "cache_values": cache_values, "page_table": page_table, "cached_lengths": cached_lengths, "req_group": req_group}


EPSILON = 1e-06
MASKED = -1e+30

def normalize(raw_rows, gain_row):
    values = raw_rows.astype(jnp.float32)
    mean_square = lax.optimization_barrier(jnp.mean(values * values, axis=-1, keepdims=True))
    return (values * lax.rsqrt(mean_square + EPSILON) * gain_row.astype(jnp.float32)[None, :]).astype(jnp.bfloat16)

def reference(q_raw, k_raw, v_new, q_gain, k_gain, cache_keys, cache_values, page_table, cached_lengths, req_group):
    requests = TOKENS // NEWTOK
    capacity = CACHE_PAGES * PAGE
    queries = normalize(q_raw, q_gain).reshape(requests, NEWTOK, HEADS, HDIM)
    new_keys = normalize(k_raw, k_gain).reshape(requests, NEWTOK, HEADS, HDIM)
    new_values = v_new.reshape(requests, NEWTOK, HEADS, HDIM)
    flat_table = page_table.reshape(-1).astype(jnp.int32)
    group_keys = cache_keys[flat_table].reshape(GROUPS, capacity, HEADS, HDIM)
    group_values = cache_values[flat_table].reshape(GROUPS, capacity, HEADS, HDIM)
    positions = jnp.arange(capacity, dtype=jnp.int32)
    factor = 1.0 / math.sqrt(HDIM)

    def one_request(request):
        group_id = req_group[request]
        usable = positions < cached_lengths[group_id]
        query_block = queries[request].astype(jnp.float32)
        cached_scores = jnp.einsum('qhd,khd->hqk', query_block, group_keys[group_id].astype(jnp.float32)) * factor
        own_scores = jnp.einsum('qhd,khd->hqk', query_block, new_keys[request].astype(jnp.float32)) * factor
        cached_scores = jnp.where(usable[None, None, :], cached_scores, MASKED)
        row_top = jnp.maximum(lax.optimization_barrier(jnp.max(cached_scores, axis=2)), lax.optimization_barrier(jnp.max(own_scores, axis=2)))
        cached_weights = jnp.where(usable[None, None, :], jnp.exp(cached_scores - row_top[:, :, None]), 0.0)
        own_weights = jnp.exp(own_scores - row_top[:, :, None])
        totals = lax.optimization_barrier(jnp.sum(cached_weights, axis=2)) + lax.optimization_barrier(jnp.sum(own_weights, axis=2))
        cached_round = lax.optimization_barrier(cached_weights.astype(jnp.bfloat16)).astype(jnp.float32)
        own_round = lax.optimization_barrier(own_weights.astype(jnp.bfloat16)).astype(jnp.float32)
        numerator = jnp.einsum('hqk,khd->qhd', cached_round, group_values[group_id].astype(jnp.float32))
        numerator = numerator + jnp.einsum('hqk,khd->qhd', own_round, new_values[request].astype(jnp.float32))
        result = numerator / jnp.transpose(totals)[:, :, None]
        return result.astype(jnp.bfloat16).reshape(NEWTOK, HEADS * HDIM)
    attended = lax.map(one_request, jnp.arange(requests, dtype=jnp.int32))
    return attended.reshape(TOKENS, HEADS * HDIM)
```

```python
import functools
import math

import jax
import jax.numpy as jnp
from jax import lax
from jax.experimental import pallas as pl
from jax.experimental.pallas import tpu as pltpu
from jax.sharding import PartitionSpec as P

HDIM = 128
GROUPS = 2
NEWTOK = 256
EPSILON = 1e-06
MASKED = -1e30
FACTOR = math.log2(math.e) / math.sqrt(HDIM)
BLOCK = 4


def normalize(raw_rows, gain_row, sum_squares, full_width):
    values = raw_rows.astype(jnp.float32)
    return (
        values * lax.rsqrt(sum_squares[:, None] / full_width + EPSILON) * gain_row[None, :]
    ).astype(jnp.bfloat16)


def attend_kernel(
    per_group,
    head_block,
    order_ref,
    limit_ref,
    count_ref,
    member_ref,
    own_ref,
    q_ref,
    k_ref,
    v_ref,
    nk_ref,
    nv_ref,
    o_ref,
    lse_ref,
    top_ref,
    total_ref,
    acc_ref,
):
    group = pl.program_id(1)
    page_len = k_ref.shape[2]
    own_rank = own_ref[group]
    full_pages = count_ref[group, 0]
    valid_pages = count_ref[group, 1]
    members = [member_ref[group, i] for i in range(per_group)]
    lanes = per_group * NEWTOK
    heads = [slice(j * HDIM, (j + 1) * HDIM) for j in range(head_block)]

    def query(j):
        return jnp.concatenate([q_ref[m, :, heads[j]] for m in members], axis=0)

    def scores_of(keys, j):
        return lax.dot_general(
            keys, query(j), (((1,), (1,)), ((), ())), preferred_element_type=jnp.float32
        )

    def mix_of(values, weights):
        return lax.dot_general(
            values,
            weights.astype(jnp.bfloat16),
            (((0,), (0,)), ((), ())),
            preferred_element_type=jnp.float32,
        )

    mine = lax.broadcasted_iota(jnp.int32, (1, lanes), 1) // NEWTOK == own_rank
    for j in range(head_block):
        scores = jnp.where(mine, scores_of(nk_ref[:, heads[j]], j), MASKED)
        top = jnp.max(scores, axis=0, keepdims=True)
        weights = jnp.where(mine, jnp.exp2(scores * FACTOR - top * FACTOR), 0.0)
        top_ref[j] = top
        total_ref[j] = jnp.sum(weights, axis=0, keepdims=True)
        acc_ref[j] = mix_of(nv_ref[:, heads[j]], weights)

    def update(pages, masked, limit):
        for j in range(head_block):
            keys = jnp.concatenate([k_ref[0, p, :, heads[j]] for p in pages], axis=0)
            values = jnp.concatenate([v_ref[0, p, :, heads[j]] for p in pages], axis=0)
            scores = scores_of(keys, j)
            if masked:
                allowed = lax.broadcasted_iota(jnp.int32, scores.shape, 0) < limit
                scores = jnp.where(allowed, scores, MASKED)
            before = top_ref[j]
            top = jnp.maximum(before, jnp.max(scores, axis=0, keepdims=True))
            weights = jnp.exp2(scores * FACTOR - top * FACTOR)
            fade = jnp.exp2((before - top) * FACTOR)
            top_ref[j] = top
            total_ref[j] = total_ref[j] * fade + jnp.sum(weights, axis=0, keepdims=True)
            acc_ref[j] = acc_ref[j] * fade + mix_of(values, weights)

    blocks = full_pages // BLOCK

    def full_step(b, _):
        update([order_ref[group, b * BLOCK + i] for i in range(BLOCK)], False, None)
        return 0

    def tail_step(p, _):
        update([order_ref[group, p]], True, limit_ref[group, p])
        return 0

    lax.fori_loop(0, blocks, full_step, 0)
    lax.fori_loop(blocks * BLOCK, valid_pages, tail_step, 0)

    for j in range(head_block):
        total = total_ref[j]
        some = total > 0.0
        inverse = 1.0 / jnp.where(some, total, 1.0)
        lse = jnp.where(some, top_ref[j] * FACTOR + jnp.log2(jnp.where(some, total, 1.0)), MASKED)
        part = (acc_ref[j] * inverse).T.astype(jnp.bfloat16)
        for i, m in enumerate(members):
            o_ref[m, :, heads[j]] = part[i * NEWTOK : (i + 1) * NEWTOK]
            lse_ref[0, j, pl.ds(m, 1), :] = lse[:, i * NEWTOK : (i + 1) * NEWTOK]


def attend(all_queries, cache_keys, cache_values, new_keys, v_new, order, limit, count, members, own):
    tokens, width = all_queries.shape
    requests = tokens // NEWTOK
    per_group = requests // GROUPS
    heads = width // HDIM
    head_block = 2 if heads % 2 == 0 else 1
    head_steps = heads // head_block
    pages = cache_keys.shape[0] // GROUPS
    page_len = cache_keys.shape[1]
    tok_dev = new_keys.shape[0]
    lanes = per_group * NEWTOK
    wide = head_block * HDIM
    keys = cache_keys.reshape(GROUPS, pages, page_len, width)
    values = cache_values.reshape(GROUPS, pages, page_len, width)
    token_spec = pl.BlockSpec((requests, NEWTOK, wide), lambda h, g, *_: (0, 0, h))
    cache_spec = pl.BlockSpec((1, pages, page_len, wide), lambda h, g, *_: (g, 0, 0, h))
    own_spec = pl.BlockSpec((tok_dev, wide), lambda h, g, *_: (0, h))
    part, lse = pl.pallas_call(
        functools.partial(attend_kernel, per_group, head_block),
        out_shape=(
            jax.ShapeDtypeStruct((requests, NEWTOK, width), jnp.bfloat16),
            jax.ShapeDtypeStruct((head_steps, head_block, requests, NEWTOK), jnp.float32),
        ),
        grid_spec=pltpu.PrefetchScalarGridSpec(
            num_scalar_prefetch=5,
            grid=(head_steps, GROUPS),
            in_specs=[token_spec, cache_spec, cache_spec, own_spec, own_spec],
            out_specs=(
                token_spec,
                pl.BlockSpec((1, head_block, requests, NEWTOK), lambda h, g, *_: (h, 0, 0, 0)),
            ),
            scratch_shapes=[
                pltpu.VMEM((head_block, 1, lanes), jnp.float32),
                pltpu.VMEM((head_block, 1, lanes), jnp.float32),
                pltpu.VMEM((head_block, HDIM, lanes), jnp.float32),
            ],
        ),
        compiler_params=pltpu.CompilerParams(
            dimension_semantics=("arbitrary", "arbitrary"), vmem_limit_bytes=48 * 1024 * 1024
        ),
        name="attend",
    )(
        order,
        limit,
        count,
        members,
        own,
        all_queries.reshape(requests, NEWTOK, width),
        keys,
        values,
        new_keys,
        v_new,
    )
    return part.reshape(tokens, width), lse.reshape(heads, tokens)


def plan_pages(page_table, cached_lengths, req_group, seq_index, pages_dev, page_len, tok_dev):
    requests = req_group.shape[0]
    per_group = requests // GROUPS
    cache_pages = page_table.shape[1]
    ids = jnp.arange(requests, dtype=jnp.int32)
    same = req_group[:, None] == req_group[None, :]
    rank = jnp.sum((same & (ids[None, :] < ids[:, None])).astype(jnp.int32), axis=1)
    groups = jnp.arange(GROUPS, dtype=jnp.int32)
    chosen = (req_group[None, None, :] == groups[:, None, None]) & (
        rank[None, None, :] == jnp.arange(per_group, dtype=jnp.int32)[None, :, None]
    )
    members = jnp.sum(jnp.where(chosen, ids[None, None, :], 0), axis=2)
    own_request = seq_index * tok_dev // NEWTOK
    is_own = members == own_request
    own = jnp.sum(jnp.where(is_own, jnp.arange(per_group, dtype=jnp.int32)[None] + 1, 0), axis=1) - 1
    local = jnp.arange(pages_dev, dtype=jnp.int32)
    slots = seq_index * (GROUPS * pages_dev) + groups[:, None] * pages_dev + local[None, :]
    hits = page_table[:, None, :] == slots[:, :, None]
    logical = jnp.sum(
        jnp.where(hits, jnp.arange(cache_pages, dtype=jnp.int32)[None, None, :], 0), axis=2
    )
    limits = jnp.clip(cached_lengths[:, None] - logical * page_len, 0, page_len)
    kind = jnp.where(limits == page_len, 0, jnp.where(limits > 0, 1, 2))
    key = kind * pages_dev + local[None, :]
    place = jnp.sum((key[:, None, :] < key[:, :, None]).astype(jnp.int32), axis=2)
    at = place[:, None, :] == local[None, :, None]
    order = jnp.sum(jnp.where(at, local[None, None, :], 0), axis=2)
    limit = jnp.sum(jnp.where(at, limits[:, None, :], 0), axis=2)
    count = jnp.stack(
        [jnp.sum((kind == 0).astype(jnp.int32), axis=1), jnp.sum((kind < 2).astype(jnp.int32), axis=1)],
        axis=1,
    )
    return order, limit, count, members, own


def on_device(
    q_raw,
    k_raw,
    v_new,
    q_gain,
    k_gain,
    cache_keys,
    cache_values,
    page_table,
    cached_lengths,
    req_group,
):
    tok_dev, width = q_raw.shape
    seq_count = lax.axis_size("seq")
    full_width = width * lax.axis_size("tp")
    heads = width // HDIM
    seq_index = lax.axis_index("seq")
    raw_query = q_raw.astype(jnp.float32)
    raw_key = k_raw.astype(jnp.float32)
    query_sums, key_sums = lax.psum(
        (jnp.sum(raw_query * raw_query, axis=1), jnp.sum(raw_key * raw_key, axis=1)), "tp"
    )
    queries = normalize(q_raw, q_gain, query_sums, full_width)
    new_keys = normalize(k_raw, k_gain, key_sums, full_width)
    all_queries = lax.all_gather(queries, "seq", axis=0, tiled=True)
    plan = plan_pages(
        page_table,
        cached_lengths,
        req_group,
        seq_index,
        cache_keys.shape[0] // GROUPS,
        cache_keys.shape[1],
        tok_dev,
    )
    part, lse = attend(all_queries, cache_keys, cache_values, new_keys, v_new, *plan)
    source_part = lax.all_to_all(
        part.reshape(seq_count, tok_dev, width), "seq", split_axis=0, concat_axis=0, tiled=True
    )
    source_lse = lax.all_to_all(
        lse.T.reshape(seq_count, tok_dev, heads), "seq", split_axis=0, concat_axis=0, tiled=True
    )
    overall = jnp.max(source_lse, axis=0)
    scaling = jnp.exp2(source_lse - overall[None])
    scaling = scaling / jnp.sum(scaling, axis=0)[None]
    mixed = jnp.sum(
        source_part.astype(jnp.float32)
        * jnp.repeat(scaling, HDIM, axis=2),
        axis=0,
    )
    return mixed.astype(jnp.bfloat16)


def solution(mesh):
    return jax.shard_map(
        on_device,
        mesh=mesh,
        in_specs=(
            P("seq", "tp"),
            P("seq", "tp"),
            P("seq", "tp"),
            P("tp"),
            P("tp"),
            P("seq", None, "tp"),
            P("seq", None, "tp"),
            P(),
            P(),
            P(),
        ),
        out_specs=P("seq", "tp"),
        check_vma=False,
    )
```

```python
import functools
import math

import jax
import jax.numpy as jnp
from jax import lax
from jax.experimental import pallas as pl
from jax.experimental.pallas import tpu as pltpu
from jax.sharding import PartitionSpec as P

HDIM = 128
GROUPS = 2
NEWTOK = 256
EPSILON = 1e-06
MASKED = -1e30
FACTOR = math.log2(math.e) / math.sqrt(HDIM)
BLOCKS = (8, 2)
CHUNK_HEADS = 4


def normalize(raw_rows, gain_row, sum_squares, full_width):
    values = raw_rows.astype(jnp.float32)
    return (
        values * lax.rsqrt(sum_squares[:, None] / full_width + EPSILON) * gain_row[None, :]
    ).astype(jnp.bfloat16)


def attend_kernel(
    per_group,
    head_block,
    order_ref,
    limit_ref,
    count_ref,
    member_ref,
    own_ref,
    q_ref,
    k_ref,
    v_ref,
    nk_ref,
    nv_ref,
    o_ref,
    top_ref,
    total_ref,
    acc_ref,
    stat_ref,
):
    step = pl.program_id(0)
    group = pl.program_id(1)
    wide = head_block * HDIM
    stat_base = o_ref.shape[2] - HDIM
    own_rank = own_ref[group]
    full_pages = count_ref[group, 0]
    valid_pages = count_ref[group, 1]
    members = [member_ref[group, i] for i in range(per_group)]
    lanes = per_group * NEWTOK
    heads = [slice(j * HDIM, (j + 1) * HDIM) for j in range(head_block)]

    def query(j):
        return jnp.concatenate([q_ref[m, :, heads[j]] for m in members], axis=0)

    def scores_of(keys, j):
        return lax.dot_general(
            keys, query(j), (((1,), (1,)), ((), ())), preferred_element_type=jnp.float32
        )

    def mix_of(values, weights):
        return lax.dot_general(
            values,
            weights.astype(jnp.bfloat16),
            (((0,), (0,)), ((), ())),
            preferred_element_type=jnp.float32,
        )

    mine = lax.broadcasted_iota(jnp.int32, (1, lanes), 1) // NEWTOK == own_rank
    for j in range(head_block):
        scores = jnp.where(mine, scores_of(nk_ref[:, heads[j]], j), MASKED)
        top = jnp.max(scores, axis=0, keepdims=True)
        weights = jnp.where(mine, jnp.exp2(scores * FACTOR - top * FACTOR), 0.0)
        top_ref[j] = top
        total_ref[j] = jnp.sum(weights, axis=0, keepdims=True)
        acc_ref[j] = mix_of(nv_ref[:, heads[j]], weights)

    def update(pages, masked, limit):
        scores, values = [], []
        for j in range(head_block):
            keys = jnp.concatenate([k_ref[0, p, :, heads[j]] for p in pages], axis=0)
            values.append(jnp.concatenate([v_ref[0, p, :, heads[j]] for p in pages], axis=0))
            scores.append(scores_of(keys, j))
        if masked:
            allowed = lax.broadcasted_iota(jnp.int32, scores[0].shape, 0) < limit
            scores = [jnp.where(allowed, each, MASKED) for each in scores]
        before = [top_ref[j] for j in range(head_block)]
        tops = [
            jnp.maximum(old, jnp.max(each, axis=0, keepdims=True))
            for old, each in zip(before, scores)
        ]
        weights = [jnp.exp2((each - top) * FACTOR) for each, top in zip(scores, tops)]
        mixes = [mix_of(value, weight) for value, weight in zip(values, weights)]
        for j in range(head_block):
            fade = jnp.exp2((before[j] - tops[j]) * FACTOR)
            top_ref[j] = tops[j]
            total_ref[j] = total_ref[j] * fade + jnp.sum(weights[j], axis=0, keepdims=True)
            acc_ref[j] = acc_ref[j] * fade + mixes[j]

    done = 0
    for size in BLOCKS:
        count = (full_pages - done) // size

        def full_step(b, _, size=size, done=done):
            update([order_ref[group, done + b * size + i] for i in range(size)], False, None)
            return 0

        lax.fori_loop(0, count, full_step, 0)
        done = done + count * size

    def tail_step(p, _):
        update([order_ref[group, p]], True, limit_ref[group, p])
        return 0

    lax.fori_loop(done, valid_pages, tail_step, 0)

    @pl.when(step == 0)
    def _():
        stat_ref[group] = jnp.zeros(stat_ref.shape[1:], jnp.float32)

    for j in range(head_block):
        total = total_ref[j]
        some = total > 0.0
        safe = jnp.where(some, total, 1.0)
        lse = jnp.where(some, top_ref[j] * FACTOR + jnp.log2(safe), MASKED)
        high = lse.astype(jnp.bfloat16).astype(jnp.float32)
        stat_ref[group, pl.ds(step * head_block + j, 1), :] = high
        stat_ref[group, pl.ds(HDIM // 2 + step * head_block + j, 1), :] = lse - high
        part = (acc_ref[j] * (1.0 / safe)).T.astype(jnp.bfloat16)
        columns = pl.ds(pl.multiple_of(step * wide + j * HDIM, HDIM), HDIM)
        for i, m in enumerate(members):
            o_ref[m, :, columns] = part[i * NEWTOK : (i + 1) * NEWTOK]

    @pl.when(step == pl.num_programs(0) - 1)
    def _():
        stats = stat_ref[group].T.astype(jnp.bfloat16)
        for i, m in enumerate(members):
            o_ref[m, :, stat_base:] = stats[i * NEWTOK : (i + 1) * NEWTOK]


def attend(first_head, chunk_queries, cache_keys, cache_values, new_keys, v_new, order, limit, count, members, own):
    tokens, width = chunk_queries.shape
    full_width = cache_keys.shape[2]
    requests = tokens // NEWTOK
    per_group = requests // GROUPS
    heads = width // HDIM
    head_block = 2 if heads % 2 == 0 else 1
    head_steps = heads // head_block
    shift = first_head // head_block
    pages = cache_keys.shape[0] // GROUPS
    page_len = cache_keys.shape[1]
    tok_dev = new_keys.shape[0]
    lanes = per_group * NEWTOK
    wide = head_block * HDIM
    keys = cache_keys.reshape(GROUPS, pages, page_len, full_width)
    values = cache_values.reshape(GROUPS, pages, page_len, full_width)
    token_spec = pl.BlockSpec((requests, NEWTOK, wide), lambda h, g, *_: (0, 0, h))
    cache_spec = pl.BlockSpec((1, pages, page_len, wide), lambda h, g, *_: (g, 0, 0, h + shift))
    own_spec = pl.BlockSpec((tok_dev, wide), lambda h, g, *_: (0, h + shift))
    pairs = GROUPS * lanes * pages * page_len * heads
    part = pl.pallas_call(
        functools.partial(attend_kernel, per_group, head_block),
        out_shape=jax.ShapeDtypeStruct((requests, NEWTOK, width + HDIM), jnp.bfloat16),
        grid_spec=pltpu.PrefetchScalarGridSpec(
            num_scalar_prefetch=5,
            grid=(head_steps, GROUPS),
            in_specs=[token_spec, cache_spec, cache_spec, own_spec, own_spec],
            out_specs=pl.BlockSpec((requests, NEWTOK, width + HDIM), lambda h, g, *_: (0, 0, 0)),
            scratch_shapes=[
                pltpu.VMEM((head_block, 1, lanes), jnp.float32),
                pltpu.VMEM((head_block, 1, lanes), jnp.float32),
                pltpu.VMEM((head_block, HDIM, lanes), jnp.float32),
                pltpu.VMEM((GROUPS, HDIM, lanes), jnp.float32),
            ],
        ),
        compiler_params=pltpu.CompilerParams(
            dimension_semantics=("arbitrary", "arbitrary"), vmem_limit_bytes=48 * 1024 * 1024
        ),
        cost_estimate=pl.CostEstimate(
            flops=4 * pairs * HDIM,
            bytes_accessed=2 * GROUPS * pages * page_len * width * 2,
            transcendentals=pairs,
        ),
        name="attend",
    )(
        order,
        limit,
        count,
        members,
        own,
        chunk_queries.reshape(requests, NEWTOK, width),
        keys,
        values,
        new_keys,
        v_new,
    )
    return part.reshape(tokens, width + HDIM)


def merge_kernel(source_ref, out_ref):
    sources, _, total_width = source_ref.shape
    width = total_width - HDIM
    half = HDIM // 2
    lses = []
    for s in range(sources):
        stats = source_ref[s, :, width:].astype(jnp.float32)
        lses.append(stats[:, :half] + stats[:, half:])
    overall = functools.reduce(jnp.maximum, lses)
    scaling = [jnp.exp2(each - overall) for each in lses]
    inverse = 1.0 / functools.reduce(jnp.add, scaling)
    for h in range(width // HDIM):
        columns = slice(h * HDIM, (h + 1) * HDIM)
        mixed = None
        for s in range(sources):
            term = source_ref[s, :, columns].astype(jnp.float32) * scaling[s][:, h : h + 1]
            mixed = term if mixed is None else mixed + term
        out_ref[:, columns] = (mixed * inverse[:, h : h + 1]).astype(jnp.bfloat16)


def merge(source):
    _, rows, total_width = source.shape
    return pl.pallas_call(
        merge_kernel,
        out_shape=jax.ShapeDtypeStruct((rows, total_width - HDIM), jnp.bfloat16),
        compiler_params=pltpu.CompilerParams(vmem_limit_bytes=32 * 1024 * 1024),
        name="merge",
    )(source)


def plan_pages(page_table, cached_lengths, req_group, seq_index, pages_dev, page_len, tok_dev):
    requests = req_group.shape[0]
    per_group = requests // GROUPS
    cache_pages = page_table.shape[1]
    ids = jnp.arange(requests, dtype=jnp.int32)
    same = req_group[:, None] == req_group[None, :]
    rank = jnp.sum((same & (ids[None, :] < ids[:, None])).astype(jnp.int32), axis=1)
    groups = jnp.arange(GROUPS, dtype=jnp.int32)
    chosen = (req_group[None, None, :] == groups[:, None, None]) & (
        rank[None, None, :] == jnp.arange(per_group, dtype=jnp.int32)[None, :, None]
    )
    members = jnp.sum(jnp.where(chosen, ids[None, None, :], 0), axis=2)
    own_request = seq_index * tok_dev // NEWTOK
    is_own = members == own_request
    own = jnp.sum(jnp.where(is_own, jnp.arange(per_group, dtype=jnp.int32)[None] + 1, 0), axis=1) - 1
    local = jnp.arange(pages_dev, dtype=jnp.int32)
    slots = seq_index * (GROUPS * pages_dev) + groups[:, None] * pages_dev + local[None, :]
    hits = page_table[:, None, :] == slots[:, :, None]
    logical = jnp.sum(
        jnp.where(hits, jnp.arange(cache_pages, dtype=jnp.int32)[None, None, :], 0), axis=2
    )
    limits = jnp.clip(cached_lengths[:, None] - logical * page_len, 0, page_len)
    kind = jnp.where(limits == page_len, 0, jnp.where(limits > 0, 1, 2))
    key = kind * pages_dev + local[None, :]
    place = jnp.sum((key[:, None, :] < key[:, :, None]).astype(jnp.int32), axis=2)
    at = place[:, None, :] == local[None, :, None]
    order = jnp.sum(jnp.where(at, local[None, None, :], 0), axis=2)
    limit = jnp.sum(jnp.where(at, limits[:, None, :], 0), axis=2)
    count = jnp.stack(
        [jnp.sum((kind == 0).astype(jnp.int32), axis=1), jnp.sum((kind < 2).astype(jnp.int32), axis=1)],
        axis=1,
    )
    return order, limit, count, members, own


def on_device(
    q_raw,
    k_raw,
    v_new,
    q_gain,
    k_gain,
    cache_keys,
    cache_values,
    page_table,
    cached_lengths,
    req_group,
):
    tok_dev, width = q_raw.shape
    seq_count = lax.axis_size("seq")
    full_width = width * lax.axis_size("tp")
    heads = width // HDIM
    seq_index = lax.axis_index("seq")
    raw_query = q_raw.astype(jnp.float32)
    raw_key = k_raw.astype(jnp.float32)
    query_sums, key_sums = lax.psum(
        (jnp.sum(raw_query * raw_query, axis=1), jnp.sum(raw_key * raw_key, axis=1)), "tp"
    )
    queries = normalize(q_raw, q_gain, query_sums, full_width)
    new_keys = normalize(k_raw, k_gain, key_sums, full_width)
    chunk = CHUNK_HEADS if heads % CHUNK_HEADS == 0 else heads
    starts = list(range(0, heads, chunk))
    gathered = [
        lax.all_gather(
            queries[:, h * HDIM : (h + chunk) * HDIM], "seq", axis=0, tiled=True
        )
        for h in starts
    ]
    plan = plan_pages(
        page_table,
        cached_lengths,
        req_group,
        seq_index,
        cache_keys.shape[0] // GROUPS,
        cache_keys.shape[1],
        tok_dev,
    )
    merged = []
    for h, chunk_queries in zip(starts, gathered):
        part = attend(h, chunk_queries, cache_keys, cache_values, new_keys, v_new, *plan)
        source = lax.all_to_all(
            part.reshape(seq_count, tok_dev, part.shape[1]),
            "seq",
            split_axis=0,
            concat_axis=0,
            tiled=True,
        )
        merged.append(merge(source))
    return jnp.concatenate(merged, axis=1)


def solution(mesh):
    return jax.shard_map(
        on_device,
        mesh=mesh,
        in_specs=(
            P("seq", "tp"),
            P("seq", "tp"),
            P("seq", "tp"),
            P("tp"),
            P("tp"),
            P("seq", None, "tp"),
            P("seq", None, "tp"),
            P(),
            P(),
            P(),
        ),
        out_specs=P("seq", "tp"),
        check_vma=False,
    )
```
